512 devices in a mesh: section: 4 (over y_lo, core), dp: 128 (over y_hi, x, z).
Axes of the slice: x: 4, y: 8 (y_hi: 4, y_lo: 2; y = y_hi * 2 + y_lo), z: 8, core: 2. Of those that a mesh axis runs over, the one named last changes fastest.
Arguments:
- student: bfloat16 [65536, 1024], P(('section', 'dp')), may hold values from -6 to 6
- teacher: bfloat16 [65536, 1024], P(('section', 'dp')), may hold values from -6 to 6
Outputs:
- student_grad: bfloat16 [65536, 1024], P(('section', 'dp'))
The draws below stay inside these ranges and needn't reach their ends.
All inputs are finite; a program needn't handle non-finite values.
Results may differ from the reference program's by a relative error of at most 0.017.
Values may be sent and summed in bfloat16 or wider, within the bound.
No kernel may reach another device: no remote copies, remote signals or barrier semaphores. Data moves between devices by JAX's collectives and lax.ppermute only.
A program may use at most 64 MiB of HBM per device.

```python
import jax
import jax.numpy as jnp
from jax import lax

D = 1024
ROWS = 128
STEPS = 3
BATCH = 65536
N_SECTION = 4
N_DP = 128


def block_scale(stream_key, shape, split, low, high):
    def one(dim, blocks):
        heights = jax.random.uniform(jax.random.fold_in(jax.random.fold_in(stream_key, 6), dim), (blocks,), jnp.float32, low / len(split), high / len(split))
        return jnp.repeat(jnp.exp(heights), shape[dim] // blocks).reshape((-1,) + (1,) * (len(shape) - dim - 1))

    gain = one(*split[0])
    for cut in split[1:]:
        gain = gain * one(*cut)
    return gain


def gaussian(own_key, shape, scale, bound, split=(), held_as=jnp.bfloat16):
    values = scale * jax.random.normal(own_key, shape, jnp.float32)
    if split:
        values = values * block_scale(own_key, shape, split, -0.22, 0.18)
    return jnp.clip(values, -bound, bound).astype(held_as)


def setup_inputs(seed: int = 0) -> dict:
    streams_of = jax.random.split(jax.random.key(seed), 3)
    return {
        "student": gaussian(streams_of[0], (BATCH, D), 1.0, 6.0, ((0, 512),)),
        "teacher": gaussian(streams_of[1], (BATCH, D), 1.0, 6.0, ((0, 512),)),
    }


def unit_rows(rows):
    values = rows.astype(jnp.float32)
    inverse = lax.rsqrt(lax.optimization_barrier(jnp.sum(values * values, axis=1, keepdims=True)) + 1e-06)
    return ((values * inverse).astype(jnp.bfloat16), inverse)

def grouped(rows):
    return rows.reshape(N_SECTION, N_DP, ROWS, D).transpose(1, 0, 2, 3).reshape(N_DP, N_SECTION * ROWS, D)

def ungrouped(rows):
    return rows.reshape(N_DP, N_SECTION, ROWS, D).transpose(1, 0, 2, 3).reshape(N_SECTION * N_DP * ROWS, D)

def reference(student, teacher):
    unit_s, inv_s = unit_rows(student)
    unit_t, unused = unit_rows(teacher)
    group_s = grouped(unit_s).astype(jnp.float32)
    group_t = grouped(unit_t).astype(jnp.float32)
    gsum = jnp.zeros(group_s.shape, jnp.float32)
    for step in range(STEPS):
        partner_s = jnp.roll(group_s, step, axis=0)
        partner_t = jnp.roll(group_t, step, axis=0)
        diff = jnp.einsum('npf,nqf->npq', group_s, partner_s) - jnp.einsum('npf,nqf->npq', group_t, partner_t)
        weights = diff.astype(jnp.bfloat16).astype(jnp.float32)
        gsum = gsum + jnp.einsum('npq,nqf->npf', weights, partner_s)
        backward = jnp.einsum('npq,npf->nqf', weights, group_s)
        gsum = gsum + jnp.roll(backward, -step, axis=0)
    total = ungrouped(gsum)
    unit_f = unit_s.astype(jnp.float32)
    along = lax.optimization_barrier(jnp.sum(unit_f * total, axis=1, keepdims=True))
    return (D / 2.0 * inv_s * (total - unit_f * along)).astype(jnp.bfloat16)
```

```python
import jax
import jax.numpy as jnp
from jax import lax
from jax.experimental import pallas as pl
from jax.experimental.pallas import tpu as pltpu
from jax.sharding import PartitionSpec as P

D = 1024
ROWS = 128
N_SECTION = 4
N_DP = 128
RUN = 32
F32 = jnp.float32
BF16 = jnp.bfloat16
VMEM = pl.BlockSpec(memory_space=pltpu.VMEM)
ROW_BY_ROW = (((1,), (1,)), ((), ()))


def route(block, target):
    pairs = []
    for q in range(N_SECTION):
        for d in range(N_DP):
            goal = target(q, d)
            if goal is not None:
                pairs.append((q * N_DP + d, goal[0] * N_DP + goal[1] % N_DP))
    return lax.ppermute(block, ("section", "dp"), pairs)


def to_core(q, d):
    return q ^ 1, d


def to_y(q, d):
    return q ^ 2, d


def along(q, d):
    return q, d + 1 - 2 * (q % 2)


def along_inside(q, d):
    last = RUN - 1 if q % 2 == 0 else 0
    return None if d % RUN == last else along(q, d)


def across(q, d):
    if q % 2 == 0:
        return (q, d + 2) if d % RUN == RUN - 2 else None
    return (q, d - 2) if d % RUN == 1 else None


def call(kernel, out_shape, flops, *operands):
    size = sum(x.size * x.dtype.itemsize for x in operands)
    return pl.pallas_call(
        kernel,
        out_shape=out_shape,
        in_specs=[VMEM] * len(operands),
        out_specs=jax.tree.map(lambda _: VMEM, out_shape),
        cost_estimate=pl.CostEstimate(flops=flops, bytes_accessed=size, transcendentals=0),
        compiler_params=pltpu.CompilerParams(vmem_limit_bytes=40 * 2**20),
    )(*operands)


def unit_kernel(s_ref, t_ref, unit_ref, inv_ref):
    for i, ref in enumerate((s_ref, t_ref)):
        values = ref[...].astype(F32)
        inverse = lax.rsqrt(jnp.sum(values * values, axis=1, keepdims=True) + 1e-06)
        unit_ref[i * ROWS : (i + 1) * ROWS, :] = (values * inverse).astype(BF16)
        if i == 0:
            inv_ref[...] = inverse


def add_terms(group, rows, factor):
    s_rows, t_rows = rows[:ROWS], rows[ROWS:]
    terms = []
    for part in group:
        diff = lax.dot_general(part[:ROWS], s_rows, ROW_BY_ROW, preferred_element_type=F32)
        diff = diff - lax.dot_general(part[ROWS:], t_rows, ROW_BY_ROW, preferred_element_type=F32)
        weights = (factor * diff).astype(BF16)
        terms.append(jnp.dot(weights, s_rows, preferred_element_type=F32))
    return terms


def first_kernel(own, sib, far, cross, one_a, one_b, sum_ref):
    group = [own[...], sib[...], far[...], cross[...]]
    total = add_terms(group, own[...], 2.0)
    for rows in (one_a, one_b):
        total = [x + y for x, y in zip(total, add_terms(group, rows[...], 1.0))]
    for i, x in enumerate(total):
        sum_ref[i * ROWS : (i + 1) * ROWS, :] = x


def second_kernel(own, sib, far, cross, two_a, two_b, sum_ref, keep_ref, send_ref):
    group = [own[...], sib[...], far[...], cross[...]]
    total = [sum_ref[i * ROWS : (i + 1) * ROWS, :] for i in range(4)]
    for rows in (two_a, two_b):
        total = [x + y for x, y in zip(total, add_terms(group, rows[...], 1.0))]
    keep_ref[:ROWS, :] = total[0]
    keep_ref[ROWS:, :] = total[2]
    send_ref[:ROWS, :] = total[1].astype(BF16)
    send_ref[ROWS:, :] = total[3].astype(BF16)


def far_kernel(keep, got, send_ref):
    send_ref[...] = (keep[ROWS:, :] + got[ROWS:, :].astype(F32)).astype(BF16)


def last_kernel(unit, inv, keep, got, got_far, out_ref):
    total = keep[:ROWS, :] + got[:ROWS, :].astype(F32) + got_far[...].astype(F32)
    unit_f = unit[:ROWS, :].astype(F32)
    along_unit = jnp.sum(unit_f * total, axis=1, keepdims=True)
    out_ref[...] = (D / 2.0 * inv[...] * (total - unit_f * along_unit)).astype(BF16)


def on_device(student, teacher):
    shape = jax.ShapeDtypeStruct
    own, inv = call(
        unit_kernel, (shape((2 * ROWS, D), BF16), shape((ROWS, 1), F32)), 10 * ROWS * D, student, teacher
    )
    one_a = route(own, along)
    sib = route(own, to_core)
    direct_a = route(own, across)
    far = route(own, to_y)
    one_b = route(sib, along)
    direct_b = route(sib, across)
    two_a = route(one_a, along_inside)
    two_b = route(one_b, along_inside)
    cross = route(far, to_core)
    core = lax.axis_index("section") % 2
    place = lax.axis_index("dp") % RUN
    at_start = place == jnp.where(core == 0, 0, RUN - 1)
    two_a = jnp.where(at_start, direct_a, two_a)
    two_b = jnp.where(at_start, direct_b, two_b)
    gram = 2 * 3 * 4 * ROWS * ROWS * D
    partial = call(first_kernel, shape((4 * ROWS, D), F32), 3 * gram, own, sib, far, cross, one_a, one_b)
    keep, send = call(
        second_kernel,
        (shape((2 * ROWS, D), F32), shape((2 * ROWS, D), BF16)),
        2 * gram,
        own, sib, far, cross, two_a, two_b, partial,
    )
    got = route(send, to_core)
    send_far = call(far_kernel, shape((ROWS, D), BF16), ROWS * D, keep, got)
    got_far = route(send_far, to_y)
    return call(last_kernel, shape((ROWS, D), BF16), 8 * ROWS * D, own, inv, keep, got, got_far)


def solution(mesh):
    placed = (P(("section", "dp"), None), P(("section", "dp"), None))
    return jax.shard_map(
        on_device, mesh=mesh, in_specs=placed, out_specs=P(("section", "dp"), None), check_vma=False
    )
```

```python
import jax
import jax.numpy as jnp
from jax import lax
from jax.experimental import pallas as pl
from jax.experimental.pallas import tpu as pltpu
from jax.sharding import PartitionSpec as P

D = 1024
ROWS = 128
N_SECTION = 4
N_DP = 128
RUN = 32
F32 = jnp.float32
BF16 = jnp.bfloat16
C1 = 400000000
C2 = 800000000
C3 = 1
C4 = 400000000
C5 = 400000000
C6 = 800000000
C7 = 400000000
C9 = 100000000
C10 = 100000000
C12 = 400000000
C11 = 800000000
C8 = 800000000
VMEM = pl.BlockSpec(memory_space=pltpu.VMEM)
ROW_BY_ROW = (((1,), (1,)), ((), ()))


def route(block, target):
    pairs = []
    for q in range(N_SECTION):
        for d in range(N_DP):
            goal = target(q, d)
            if goal is not None:
                pairs.append((q * N_DP + d, goal[0] * N_DP + goal[1] % N_DP))
    return lax.ppermute(block, ("section", "dp"), pairs)


def to_core(q, d):
    return q ^ 1, d


def to_y(q, d):
    return q ^ 2, d


def along(q, d):
    return q, d + 1 - 2 * (q % 2)


def along_inside(q, d):
    last = RUN - 1 if q % 2 == 0 else 0
    return None if d % RUN == last else along(q, d)


def across(q, d):
    if q % 2 == 0:
        return (q, d + 2) if d % RUN == RUN - 2 else None
    return (q, d - 2) if d % RUN == 1 else None


def aside(q, d):
    if q % 2 == 1:
        return (q ^ 1, d - 24) if d % RUN in (RUN - 2, RUN - 1) else None
    return (q ^ 1, d + 24) if d % RUN in (0, 1) else None


def from_aside(q, d):
    if q % 2 == 0:
        return {7: (q, d + 25), 6: (q ^ 1, d + 26)}.get(d % RUN)
    return {RUN - 8: (q, d - 25), RUN - 7: (q ^ 1, d - 26)}.get(d % RUN)


def call(kernel, out_shape, flops, *operands):
    size = sum(x.size * x.dtype.itemsize for x in operands)
    return pl.pallas_call(
        kernel,
        out_shape=out_shape,
        in_specs=[pl.BlockSpec(memory_space=pltpu.SMEM) if x.ndim == 1 else VMEM for x in operands],
        out_specs=jax.tree.map(lambda _: VMEM, out_shape),
        cost_estimate=pl.CostEstimate(flops=flops, bytes_accessed=size, transcendentals=0),
        compiler_params=pltpu.CompilerParams(vmem_limit_bytes=40 * 2**20),
    )(*operands)


def unit_kernel(s_hbm, t_hbm, unit_ref, inv_ref, s_ref, t_ref, sems):
    copies = [
        pltpu.make_async_copy(src, dst, sems.at[i])
        for i, (src, dst) in enumerate(((s_hbm, s_ref), (t_hbm, t_ref)))
    ]
    for copy in copies:
        copy.start()
    for i, ref in enumerate((s_ref, t_ref)):
        copies[i].wait()
        values = ref[...].astype(F32)
        inverse = lax.rsqrt(jnp.sum(values * values, axis=1, keepdims=True) + 1e-06)
        unit_ref[i * ROWS : (i + 1) * ROWS, :] = (values * inverse).astype(BF16)
        if i == 0:
            inv_ref[...] = inverse


def unit_rows(student, teacher):
    return pl.pallas_call(
        unit_kernel,
        out_shape=(jax.ShapeDtypeStruct((2 * ROWS, D), BF16), jax.ShapeDtypeStruct((ROWS, 1), F32)),
        in_specs=[pl.BlockSpec(memory_space=pl.ANY)] * 2,
        out_specs=(VMEM, VMEM),
        scratch_shapes=[pltpu.VMEM((ROWS, D), BF16)] * 2 + [pltpu.SemaphoreType.DMA((2,))],
        cost_estimate=pl.CostEstimate(flops=10 * ROWS * D, bytes_accessed=4 * ROWS * D, transcendentals=0),
        compiler_params=pltpu.CompilerParams(vmem_limit_bytes=40 * 2**20),
    )(student, teacher)


def stack(blocks, part):
    return jnp.concatenate([x[part * ROWS : (part + 1) * ROWS, :] for x in blocks], axis=0)


def terms(parts, rows, own_first):
    s_rows, t_rows = stack(rows, 0), stack(rows, 1)
    diff = lax.dot_general(stack(parts, 0), s_rows, ROW_BY_ROW, preferred_element_type=F32)
    diff = diff - lax.dot_general(stack(parts, 1), t_rows, ROW_BY_ROW, preferred_element_type=F32)
    if own_first:
        diff = jnp.concatenate([2.0 * diff[:, :ROWS], diff[:, ROWS:]], axis=1)
    return jnp.dot(diff.astype(BF16), s_rows, preferred_element_type=F32)


def hold_kernel(block, out_ref):
    out_ref[...] = block[...]


def mix_kernel(flag, one_b, near_b, direct, next_ref, extra_ref):
    at_end = flag[0] == 1
    none = jnp.zeros_like(near_b)
    next_ref[...] = one_b[...] + jnp.where(at_end, near_b[...], none)
    extra_ref[...] = direct[...] + jnp.where(at_end, none, near_b[...])


def first_kernel(one, other, own, one_a, one_b, two_a, sum_ref):
    sum_ref[...] = terms([one, other], [own, one_a, one_b, two_a], True)


def final_kernel(one, other, two, extra, old_ref, keep_ref, send_ref):
    total = old_ref[...] + terms([one, other], [two, extra], False)
    keep_ref[...] = total[:ROWS, :]
    send_ref[...] = total[ROWS:, :].astype(BF16)


def far_kernel(keep, got, send_ref):
    send_ref[...] = (keep[...] + got[...].astype(F32)).astype(BF16)


def last_kernel(unit, inv, keep, got, got_far, out_ref):
    total = keep[...] + got[...].astype(F32) + got_far[...].astype(F32)
    unit_f = unit[:ROWS, :].astype(F32)
    along_unit = jnp.sum(unit_f * total, axis=1, keepdims=True)
    out_ref[...] = (D / 2.0 * inv[...] * (total - unit_f * along_unit)).astype(BF16)


def after(block, *others):
    return lax.optimization_barrier((block, *others))[0]


def hold(block, cost):
    return call(hold_kernel, jax.ShapeDtypeStruct(block.shape, block.dtype), cost, block)


def on_device(student, teacher):
    shape = jax.ShapeDtypeStruct
    quarter_f, quarter_h = shape((ROWS, D), F32), shape((ROWS, D), BF16)
    half, both = shape((2 * ROWS, D), F32), shape((2 * ROWS, D), BF16)
    gram = 2 * 3 * 2 * ROWS * ROWS * D
    own, inv = unit_rows(student, teacher)
    one_a = hold(route(own, along), C9)
    spread = route(own, aside)
    direct = hold(route(own, across), C11)
    far = hold(route(own, to_y), C6)
    sib = route(own, to_core)
    one_b = route(sib, along_inside)
    near_b = hold(route(spread, from_aside), C12)
    core = lax.axis_index("section") % 2
    place = lax.axis_index("dp") % RUN
    flag = (place == core * (RUN - 1)).astype(jnp.int32).reshape(1)
    one_b, extra = call(mix_kernel, (both, both), C1, flag, after(one_b, far), near_b, direct)
    two_a = hold(route(one_a, along_inside), C5)
    two_b = hold(route(one_b, along_inside), C2)
    near_sum = call(first_kernel, half, C8, own, sib, own, one_a, after(one_b, far), two_a)
    cross = route(after(far, one_b), to_core)
    away_sum = call(first_kernel, half, 0, far, cross, own, one_a, one_b, two_a)
    keep_far, send_far = call(
        final_kernel, (quarter_f, quarter_h), C4, far, cross, two_b, extra, away_sum
    )
    got_far = route(send_far, to_core)
    send_far = call(far_kernel, quarter_h, ROWS * D, keep_far, got_far)
    got_far = hold(route(send_far, to_y), C10)
    keep, send = call(final_kernel, (quarter_f, quarter_h), gram, own, sib, two_b, extra, near_sum)
    got = route(after(send, send_far), to_core)
    return call(last_kernel, quarter_h, 8 * ROWS * D, own, inv, keep, got, got_far)


def solution(mesh):
    placed = (P(("section", "dp"), None), P(("section", "dp"), None))
    return jax.shard_map(
        on_device, mesh=mesh, in_specs=placed, out_specs=P(("section", "dp"), None), check_vma=False
    )
```

```python
import jax
import jax.numpy as jnp
from jax import lax
from jax.experimental import pallas as pl
from jax.experimental.pallas import tpu as pltpu
from jax.sharding import PartitionSpec as P

D = 1024
ROWS = 128
N_SECTION = 4
N_DP = 128
RUN = 32
F32 = jnp.float32
BF16 = jnp.bfloat16
C1 = 400000000
C2 = 400000000
C3 = 1
C4 = 400000000
C5 = 6400000000
C6 = 100000000
C7 = 800000000
C9 = 400000000
C10 = 200000000
C15 = 1600000000
C14 = 6400000000
C13 = 400000000
C12 = 200000000
C11 = 400000000
C8 = 400000000
VMEM = pl.BlockSpec(memory_space=pltpu.VMEM)
ROW_BY_ROW = (((1,), (1,)), ((), ()))


def route(block, target):
    pairs = []
    for q in range(N_SECTION):
        for d in range(N_DP):
            goal = target(q, d)
            if goal is not None:
                pairs.append((q * N_DP + d, goal[0] * N_DP + goal[1] % N_DP))
    return lax.ppermute(block, ("section", "dp"), pairs)


def to_core(q, d):
    return q ^ 1, d


def to_y(q, d):
    return q ^ 2, d


def along(q, d):
    return q, d + 1 - 2 * (q % 2)


def along_inside(q, d):
    last = RUN - 1 if q % 2 == 0 else 0
    return None if d % RUN == last else along(q, d)


def across(q, d):
    if q % 2 == 0:
        return (q, d + 2) if d % RUN == RUN - 2 else None
    return (q, d - 2) if d % RUN == 1 else None


def aside(q, d):
    if q % 2 == 1:
        return (q ^ 1, d - 24) if d % RUN in (RUN - 2, RUN - 1) else None
    return (q ^ 1, d + 24) if d % RUN in (0, 1) else None


def from_aside(q, d):
    if q % 2 == 0:
        return {7: (q, d + 25), 6: (q ^ 1, d + 26)}.get(d % RUN)
    return {RUN - 8: (q, d - 25), RUN - 7: (q ^ 1, d - 26)}.get(d % RUN)


def call(kernel, out_shape, flops, *operands):
    size = sum(x.size * x.dtype.itemsize for x in operands)
    return pl.pallas_call(
        kernel,
        out_shape=out_shape,
        in_specs=[pl.BlockSpec(memory_space=pltpu.SMEM) if x.ndim == 1 else VMEM for x in operands],
        out_specs=jax.tree.map(lambda _: VMEM, out_shape),
        cost_estimate=pl.CostEstimate(flops=flops, bytes_accessed=size, transcendentals=0),
        compiler_params=pltpu.CompilerParams(vmem_limit_bytes=16 * 2**20),
    )(*operands)


def unit_kernel(s_hbm, t_hbm, unit_ref, inv_ref, s_ref, t_ref, sems):
    copies = [
        pltpu.make_async_copy(src, dst, sems.at[i])
        for i, (src, dst) in enumerate(((s_hbm, s_ref), (t_hbm, t_ref)))
    ]
    for copy in copies:
        copy.start()
    for i, ref in enumerate((s_ref, t_ref)):
        copies[i].wait()
        values = ref[...].astype(F32)
        inverse = lax.rsqrt(jnp.sum(values * values, axis=1, keepdims=True) + 1e-06)
        unit_ref[i * ROWS : (i + 1) * ROWS, :] = (values * inverse).astype(BF16)
        if i == 0:
            inv_ref[...] = inverse


def unit_rows(student, teacher):
    return pl.pallas_call(
        unit_kernel,
        out_shape=(jax.ShapeDtypeStruct((2 * ROWS, D), BF16), jax.ShapeDtypeStruct((ROWS, 1), F32)),
        in_specs=[pl.BlockSpec(memory_space=pl.ANY)] * 2,
        out_specs=(VMEM, VMEM),
        scratch_shapes=[pltpu.VMEM((ROWS, D), BF16)] * 2 + [pltpu.SemaphoreType.DMA((2,))],
        cost_estimate=pl.CostEstimate(flops=10 * ROWS * D, bytes_accessed=4 * ROWS * D, transcendentals=0),
        compiler_params=pltpu.CompilerParams(vmem_limit_bytes=16 * 2**20),
    )(student, teacher)


def stack(blocks, part):
    return jnp.concatenate([x[part * ROWS : (part + 1) * ROWS, :] for x in blocks], axis=0)


def terms(parts, rows, own_first):
    s_rows, t_rows = stack(rows, 0), stack(rows, 1)
    diff = lax.dot_general(stack(parts, 0), s_rows, ROW_BY_ROW, preferred_element_type=F32)
    diff = diff - lax.dot_general(stack(parts, 1), t_rows, ROW_BY_ROW, preferred_element_type=F32)
    if own_first:
        diff = jnp.concatenate([2.0 * diff[:, :ROWS], diff[:, ROWS:]], axis=1)
    return jnp.dot(diff.astype(BF16), s_rows, preferred_element_type=F32)


def hold_kernel(block, out_ref):
    out_ref[...] = block[...]


def next_kernel(flag, one_b, near_b, rows_ref):
    rows_ref[...] = one_b[...] + jnp.where(flag[0] == 1, near_b[...], jnp.zeros_like(near_b))


def extra_kernel(flag, near_b, direct, rows_ref):
    rows_ref[...] = direct[...] + jnp.where(flag[0] == 1, jnp.zeros_like(near_b), near_b[...])


def first_kernel(one, other, own, one_a, one_b, two_a, sum_ref):
    sum_ref[...] = terms([one, other], [own, one_a, one_b, two_a], True)


def final_kernel(one, other, two, extra, old_ref, keep_ref, send_ref):
    total = old_ref[...] + terms([one, other], [two, extra], False)
    keep_ref[...] = total[:ROWS, :]
    send_ref[...] = total[ROWS:, :].astype(BF16)


def far_kernel(keep, got, send_ref):
    send_ref[...] = (keep[...] + got[...].astype(F32)).astype(BF16)


def last_kernel(unit, inv, keep, got, got_far, out_ref):
    total = keep[...] + got[...].astype(F32) + got_far[...].astype(F32)
    unit_f = unit[:ROWS, :].astype(F32)
    along_unit = jnp.sum(unit_f * total, axis=1, keepdims=True)
    out_ref[...] = (D / 2.0 * inv[...] * (total - unit_f * along_unit)).astype(BF16)


def after(block, *others):
    return lax.optimization_barrier((block, *others))[0]


def hold(block, cost):
    return call(hold_kernel, jax.ShapeDtypeStruct(block.shape, block.dtype), cost, block)


def on_device(student, teacher):
    shape = jax.ShapeDtypeStruct
    quarter_f, quarter_h = shape((ROWS, D), F32), shape((ROWS, D), BF16)
    half, both = shape((2 * ROWS, D), F32), shape((2 * ROWS, D), BF16)
    gram = 2 * 3 * 2 * ROWS * ROWS * D
    own, inv = unit_rows(student, teacher)
    one_a = hold(route(own, along), C9)
    spread = hold(route(own, aside), C13)
    direct = hold(route(own, across), C11)
    far = hold(route(after(own, spread), to_y), C6)
    sib = route(own, to_core)
    one_b = hold(route(sib, along_inside), C15)
    near_b = route(spread, from_aside)
    core = lax.axis_index("section") % 2
    place = lax.axis_index("dp") % RUN
    flag = (place == core * (RUN - 1)).astype(jnp.int32).reshape(1)
    one_b = call(next_kernel, both, C1, flag, one_b, near_b)
    extra = call(extra_kernel, both, C7, flag, near_b, direct)
    two_a = hold(route(one_a, along_inside), C5)
    two_b = route(one_b, along_inside)
    near_sum = call(first_kernel, half, C8, own, sib, own, one_a, after(one_b, far), two_a)
    cross = route(after(far, one_b, extra), to_core)
    away_sum = call(first_kernel, half, C14, far, cross, own, one_a, one_b, two_a)
    keep_far, send_far = call(
        final_kernel, (quarter_f, quarter_h), C4, far, cross, two_b, extra, away_sum
    )
    got_far = route(send_far, to_core)
    send_far = call(far_kernel, quarter_h, ROWS * D, keep_far, got_far)
    got_far = hold(route(send_far, to_y), C10)
    keep, send = call(final_kernel, (quarter_f, quarter_h), gram, own, sib, two_b, extra, near_sum)
    got = route(after(send, send_far), to_core)
    return call(last_kernel, quarter_h, 8 * ROWS * D, own, inv, keep, got, got_far)


def solution(mesh):
    placed = (P(("section", "dp"), None), P(("section", "dp"), None))
    return jax.shard_map(
        on_device, mesh=mesh, in_specs=placed, out_specs=P(("section", "dp"), None), check_vma=False
    )
```

```python
import jax
import jax.numpy as jnp
from jax import lax
from jax.experimental import pallas as pl
from jax.experimental.pallas import tpu as pltpu
from jax.sharding import PartitionSpec as P

D = 1024
ROWS = 128
N_SECTION = 4
N_DP = 128
RUN = 32
F32 = jnp.float32
BF16 = jnp.bfloat16
C1 = 400000000
C2 = 400000000
C3 = 1
C4 = 400000000
C5 = 6400000000
C6 = 100000000
C7 = 800000000
C9 = 400000000
C10 = 200000000
C15 = 1600000000
C14 = 6400000000
C13 = 400000000
C12 = 200000000
C11 = 400000000
C8 = 400000000
VMEM = pl.BlockSpec(memory_space=pltpu.VMEM)
ROW_BY_ROW = (((1,), (1,)), ((), ()))


def route(block, target):
    pairs = []
    for q in range(N_SECTION):
        for d in range(N_DP):
            goal = target(q, d)
            if goal is not None:
                pairs.append((q * N_DP + d, goal[0] * N_DP + goal[1] % N_DP))
    return lax.ppermute(block, ("section", "dp"), pairs)


def to_core(q, d):
    return q ^ 1, d


def to_y(q, d):
    return q ^ 2, d


def along(q, d):
    return q, d + 1 - 2 * (q % 2)


def along_inside(q, d):
    last = RUN - 1 if q % 2 == 0 else 0
    return None if d % RUN == last else along(q, d)


def across(q, d):
    if q % 2 == 0:
        return (q, d + 2) if d % RUN == RUN - 2 else None
    return (q, d - 2) if d % RUN == 1 else None


def aside(q, d):
    step = 24 if q < 2 else 7
    if q % 2 == 1:
        steps = {RUN - 1: -step, RUN - 2: -24}
        return (q, d + steps[d % RUN]) if d % RUN in steps else None
    steps = {0: step, 1: 24}
    return (q ^ 1, d + steps[d % RUN]) if d % RUN in steps else None


def from_aside(q, d):
    if q % 2 == 0:
        return None
    step = 24 if q < 2 else 7
    goals = {
        RUN - 1 - step: (q ^ 1, d + step + 1),
        step: (q, d - step - 1),
        6: (q, d + 26),
        25: (q ^ 1, d - 26),
    }
    return goals.get(d % RUN)


def call(kernel, out_shape, flops, *operands):
    size = sum(x.size * x.dtype.itemsize for x in operands)
    return pl.pallas_call(
        kernel,
        out_shape=out_shape,
        in_specs=[pl.BlockSpec(memory_space=pltpu.SMEM) if x.ndim == 1 else VMEM for x in operands],
        out_specs=jax.tree.map(lambda _: VMEM, out_shape),
        cost_estimate=pl.CostEstimate(flops=flops, bytes_accessed=size, transcendentals=0),
        compiler_params=pltpu.CompilerParams(vmem_limit_bytes=16 * 2**20),
    )(*operands)


def unit_kernel(s_hbm, t_hbm, unit_ref, inv_ref, s_ref, t_ref, sems):
    copies = [
        pltpu.make_async_copy(src, dst, sems.at[i])
        for i, (src, dst) in enumerate(((s_hbm, s_ref), (t_hbm, t_ref)))
    ]
    for copy in copies:
        copy.start()
    for i, ref in enumerate((s_ref, t_ref)):
        copies[i].wait()
        values = ref[...].astype(F32)
        inverse = lax.rsqrt(jnp.sum(values * values, axis=1, keepdims=True) + 1e-06)
        unit_ref[i * ROWS : (i + 1) * ROWS, :] = (values * inverse).astype(BF16)
        if i == 0:
            inv_ref[...] = inverse


def unit_rows(student, teacher):
    return pl.pallas_call(
        unit_kernel,
        out_shape=(jax.ShapeDtypeStruct((2 * ROWS, D), BF16), jax.ShapeDtypeStruct((ROWS, 1), F32)),
        in_specs=[pl.BlockSpec(memory_space=pl.ANY)] * 2,
        out_specs=(VMEM, VMEM),
        scratch_shapes=[pltpu.VMEM((ROWS, D), BF16)] * 2 + [pltpu.SemaphoreType.DMA((2,))],
        cost_estimate=pl.CostEstimate(flops=10 * ROWS * D, bytes_accessed=4 * ROWS * D, transcendentals=0),
        compiler_params=pltpu.CompilerParams(vmem_limit_bytes=16 * 2**20),
    )(student, teacher)


def stack(blocks, part):
    return jnp.concatenate([x[part * ROWS : (part + 1) * ROWS, :] for x in blocks], axis=0)


def terms(parts, rows, own_first):
    s_rows, t_rows = stack(rows, 0), stack(rows, 1)
    diff = lax.dot_general(stack(parts, 0), s_rows, ROW_BY_ROW, preferred_element_type=F32)
    diff = diff - lax.dot_general(stack(parts, 1), t_rows, ROW_BY_ROW, preferred_element_type=F32)
    if own_first:
        diff = jnp.concatenate([2.0 * diff[:, :ROWS], diff[:, ROWS:]], axis=1)
    return jnp.dot(diff.astype(BF16), s_rows, preferred_element_type=F32)


def hold_kernel(block, out_ref):
    out_ref[...] = block[...]


def next_kernel(flag, one_b, near_b, rows_ref):
    rows_ref[...] = one_b[...] + jnp.where(flag[0] == 1, near_b[...], jnp.zeros_like(near_b))


def extra_kernel(flag, near_b, direct, rows_ref):
    rows_ref[...] = direct[...] + jnp.where(flag[0] == 1, jnp.zeros_like(near_b), near_b[...])


def first_kernel(one, other, own, one_a, one_b, two_a, sum_ref):
    sum_ref[...] = terms([one, other], [own, one_a, one_b, two_a], True)


def final_kernel(one, other, two, extra, old_ref, keep_ref, send_ref):
    total = old_ref[...] + terms([one, other], [two, extra], False)
    keep_ref[...] = total[:ROWS, :]
    send_ref[...] = total[ROWS:, :].astype(BF16)


def far_kernel(keep, got, send_ref):
    send_ref[...] = (keep[...] + got[...].astype(F32)).astype(BF16)


def last_kernel(unit, inv, keep, got, got_far, out_ref):
    total = keep[...] + got[...].astype(F32) + got_far[...].astype(F32)
    unit_f = unit[:ROWS, :].astype(F32)
    along_unit = jnp.sum(unit_f * total, axis=1, keepdims=True)
    out_ref[...] = (D / 2.0 * inv[...] * (total - unit_f * along_unit)).astype(BF16)


def after(block, *others):
    return lax.optimization_barrier((block, *others))[0]


def hold(block, cost):
    return call(hold_kernel, jax.ShapeDtypeStruct(block.shape, block.dtype), cost, block)


def on_device(student, teacher):
    shape = jax.ShapeDtypeStruct
    quarter_f, quarter_h = shape((ROWS, D), F32), shape((ROWS, D), BF16)
    half, both = shape((2 * ROWS, D), F32), shape((2 * ROWS, D), BF16)
    gram = 2 * 3 * 2 * ROWS * ROWS * D
    own, inv = unit_rows(student, teacher)
    one_a = hold(route(own, along), C9)
    spread = hold(route(own, aside), C13)
    direct = hold(route(own, across), C11)
    far = hold(route(after(own, spread), to_y), C6)
    sib = route(own, to_core)
    one_b = hold(route(sib, along_inside), C15)
    near_b = route(spread, from_aside)
    core = lax.axis_index("section") % 2
    place = lax.axis_index("dp") % RUN
    flag = (place == core * (RUN - 1)).astype(jnp.int32).reshape(1)
    one_b = call(next_kernel, both, C1, flag, one_b, near_b)
    extra = call(extra_kernel, both, C7, flag, near_b, direct)
    two_a = hold(route(one_a, along_inside), C5)
    two_b = route(one_b, along_inside)
    near_sum = call(first_kernel, half, C8, own, sib, own, one_a, after(one_b, far), two_a)
    cross = route(after(far, one_b, extra), to_core)
    away_sum = call(first_kernel, half, C14, far, cross, own, one_a, one_b, two_a)
    keep_far, send_far = call(
        final_kernel, (quarter_f, quarter_h), C4, far, cross, two_b, extra, away_sum
    )
    got_far = route(send_far, to_core)
    send_far = call(far_kernel, quarter_h, ROWS * D, keep_far, got_far)
    got_far = hold(route(send_far, to_y), C10)
    keep, send = call(final_kernel, (quarter_f, quarter_h), gram, own, sib, two_b, extra, near_sum)
    got = route(after(send, send_far), to_core)
    return call(last_kernel, quarter_h, 8 * ROWS * D, own, inv, keep, got, got_far)


def solution(mesh):
    placed = (P(("section", "dp"), None), P(("section", "dp"), None))
    return jax.shard_map(
        on_device, mesh=mesh, in_specs=placed, out_specs=P(("section", "dp"), None), check_vma=False
    )
```

```python
import jax
import jax.numpy as jnp
from jax import lax
from jax.experimental import pallas as pl
from jax.experimental.pallas import tpu as pltpu
from jax.sharding import PartitionSpec as P

D = 1024
ROWS = 128
N_SECTION = 4
N_DP = 128
RUN = 32
F32 = jnp.float32
BF16 = jnp.bfloat16
NEXT_COST = 400_000_000
FINAL_COST = 400_000_000
TWO_A_COST = 6_400_000_000
FAR_COST = 100_000_000
EXTRA_COST = 800_000_000
ONE_A_COST = 400_000_000
TAIL_COST = 200_000_000
AWAY_COST = 6_400_000_000
SPREAD_COST = 400_000_000
DIRECT_COST = 400_000_000
NEAR_COST = 400_000_000
VMEM = pl.BlockSpec(memory_space=pltpu.VMEM)
ROW_BY_ROW = (((1,), (1,)), ((), ()))


def route(block, target):
    pairs = []
    for q in range(N_SECTION):
        for d in range(N_DP):
            goal = target(q, d)
            if goal is not None:
                pairs.append((q * N_DP + d, goal[0] * N_DP + goal[1] % N_DP))
    return lax.ppermute(block, ("section", "dp"), pairs)


def to_core(q, d):
    return q ^ 1, d


def to_y(q, d):
    return q ^ 2, d


def along(q, d):
    return q, d + 1 - 2 * (q % 2)


def along_inside(q, d):
    last = RUN - 1 if q % 2 == 0 else 0
    return None if d % RUN == last else along(q, d)


def across(q, d):
    if q % 2 == 0:
        return (q, d + 2) if d % RUN == RUN - 2 else None
    return (q, d - 2) if d % RUN == 1 else None


def aside(q, d):
    step = 24 if q < 2 else 7
    if q % 2 == 1:
        steps = {RUN - 1: -step, RUN - 2: -24}
        return (q, d + steps[d % RUN]) if d % RUN in steps else None
    steps = {0: step, 1: 24}
    return (q ^ 1, d + steps[d % RUN]) if d % RUN in steps else None


def from_aside(q, d):
    if q % 2 == 0:
        return None
    step = 24 if q < 2 else 7
    goals = {
        RUN - 1 - step: (q ^ 1, d + step + 1),
        step: (q, d - step - 1),
        6: (q, d + 26),
        25: (q ^ 1, d - 26),
    }
    return goals.get(d % RUN)


def call(kernel, out_shape, flops, *operands):
    size = sum(x.size * x.dtype.itemsize for x in operands)
    return pl.pallas_call(
        kernel,
        out_shape=out_shape,
        in_specs=[pl.BlockSpec(memory_space=pltpu.SMEM) if x.ndim == 1 else VMEM for x in operands],
        out_specs=jax.tree.map(lambda _: VMEM, out_shape),
        cost_estimate=pl.CostEstimate(flops=flops, bytes_accessed=size, transcendentals=0),
        compiler_params=pltpu.CompilerParams(vmem_limit_bytes=16 * 2**20),
    )(*operands)


def unit_kernel(s_hbm, t_hbm, unit_ref, inv_ref, s_ref, t_ref, sems):
    copies = [
        pltpu.make_async_copy(src, dst, sems.at[i])
        for i, (src, dst) in enumerate(((s_hbm, s_ref), (t_hbm, t_ref)))
    ]
    for copy in copies:
        copy.start()
    for i, ref in enumerate((s_ref, t_ref)):
        copies[i].wait()
        values = ref[...].astype(F32)
        inverse = lax.rsqrt(jnp.sum(values * values, axis=1, keepdims=True) + 1e-06)
        unit_ref[i * ROWS : (i + 1) * ROWS, :] = (values * inverse).astype(BF16)
        if i == 0:
            inv_ref[...] = inverse


def unit_rows(student, teacher):
    return pl.pallas_call(
        unit_kernel,
        out_shape=(jax.ShapeDtypeStruct((2 * ROWS, D), BF16), jax.ShapeDtypeStruct((ROWS, 1), F32)),
        in_specs=[pl.BlockSpec(memory_space=pl.ANY)] * 2,
        out_specs=(VMEM, VMEM),
        scratch_shapes=[pltpu.VMEM((ROWS, D), BF16)] * 2 + [pltpu.SemaphoreType.DMA((2,))],
        cost_estimate=pl.CostEstimate(flops=10 * ROWS * D, bytes_accessed=4 * ROWS * D, transcendentals=0),
        compiler_params=pltpu.CompilerParams(vmem_limit_bytes=16 * 2**20),
    )(student, teacher)


def stack(blocks, part):
    return jnp.concatenate([x[part * ROWS : (part + 1) * ROWS, :] for x in blocks], axis=0)


def terms(parts, rows, own_first):
    s_rows, t_rows = stack(rows, 0), stack(rows, 1)
    diff = lax.dot_general(stack(parts, 0), s_rows, ROW_BY_ROW, preferred_element_type=F32)
    diff = diff - lax.dot_general(stack(parts, 1), t_rows, ROW_BY_ROW, preferred_element_type=F32)
    if own_first:
        diff = jnp.concatenate([2.0 * diff[:, :ROWS], diff[:, ROWS:]], axis=1)
    return jnp.dot(diff.astype(BF16), s_rows, preferred_element_type=F32)


def hold_kernel(block, out_ref):
    out_ref[...] = block[...]


def next_kernel(flag, one_b, near_b, rows_ref):
    rows_ref[...] = one_b[...] + jnp.where(flag[0] == 1, near_b[...], jnp.zeros_like(near_b))


def extra_kernel(flag, near_b, direct, rows_ref):
    rows_ref[...] = direct[...] + jnp.where(flag[0] == 1, jnp.zeros_like(near_b), near_b[...])


def first_kernel(one, other, own, one_a, one_b, two_a, sum_ref):
    sum_ref[...] = terms([one, other], [own, one_a, one_b, two_a], True)


def final_kernel(one, other, two, extra, old_ref, keep_ref, send_ref):
    total = old_ref[...] + terms([one, other], [two, extra], False)
    keep_ref[...] = total[:ROWS, :]
    send_ref[...] = total[ROWS:, :].astype(BF16)


def far_kernel(keep, got, send_ref):
    send_ref[...] = (keep[...] + got[...].astype(F32)).astype(BF16)


def last_kernel(unit, inv, keep, got, got_far, out_ref):
    total = keep[...] + got[...].astype(F32) + got_far[...].astype(F32)
    unit_f = unit[:ROWS, :].astype(F32)
    along_unit = jnp.sum(unit_f * total, axis=1, keepdims=True)
    out_ref[...] = (D / 2.0 * inv[...] * (total - unit_f * along_unit)).astype(BF16)


def after(block, *others):
    return lax.optimization_barrier((block, *others))[0]


def hold(block, cost):
    return call(hold_kernel, jax.ShapeDtypeStruct(block.shape, block.dtype), cost, block)


def on_device(student, teacher):
    shape = jax.ShapeDtypeStruct
    quarter_f, quarter_h = shape((ROWS, D), F32), shape((ROWS, D), BF16)
    half, both = shape((2 * ROWS, D), F32), shape((2 * ROWS, D), BF16)
    gram = 2 * 3 * 2 * ROWS * ROWS * D
    own, inv = unit_rows(student, teacher)
    one_a = hold(route(own, along), ONE_A_COST)
    spread = hold(route(own, aside), SPREAD_COST)
    direct = hold(route(own, across), DIRECT_COST)
    far = hold(route(after(own, spread), to_y), FAR_COST)
    sib = route(own, to_core)
    one_b = route(sib, along_inside)
    near_b = route(spread, from_aside)
    core = lax.axis_index("section") % 2
    place = lax.axis_index("dp") % RUN
    flag = (place == core * (RUN - 1)).astype(jnp.int32).reshape(1)
    one_b = call(next_kernel, both, NEXT_COST, flag, one_b, near_b)
    extra = call(extra_kernel, both, EXTRA_COST, flag, near_b, direct)
    two_a = hold(route(one_a, along_inside), TWO_A_COST)
    two_b = route(one_b, along_inside)
    near_sum = call(first_kernel, half, NEAR_COST, own, sib, own, one_a, after(one_b, far), two_a)
    cross = route(after(far, one_b, extra), to_core)
    away_sum = call(first_kernel, half, AWAY_COST, far, cross, own, one_a, one_b, two_a)
    keep_far, send_far = call(
        final_kernel, (quarter_f, quarter_h), FINAL_COST, far, cross, two_b, extra, away_sum
    )
    got_far = route(send_far, to_core)
    send_far = call(far_kernel, quarter_h, ROWS * D, keep_far, got_far)
    got_far = hold(route(send_far, to_y), TAIL_COST)
    keep, send = call(final_kernel, (quarter_f, quarter_h), gram, own, sib, two_b, extra, near_sum)
    got = route(after(send, send_far), to_core)
    return call(last_kernel, quarter_h, 8 * ROWS * D, own, inv, keep, got, got_far)


def solution(mesh):
    placed = (P(("section", "dp"), None), P(("section", "dp"), None))
    return jax.shard_map(
        on_device, mesh=mesh, in_specs=placed, out_specs=P(("section", "dp"), None), check_vma=False
    )
```

```python
import jax
import jax.numpy as jnp
from jax import lax
from jax.experimental import pallas as pl
from jax.experimental.pallas import tpu as pltpu
from jax.sharding import PartitionSpec as P

D = 1024
ROWS = 128
N_SECTION = 4
N_DP = 128
RUN = 32
PARTS = 4
F32 = jnp.float32
BF16 = jnp.bfloat16
START_COST = 1
NEXT_COST = 400_000_000
FINAL_COST = 400_000_000
TWO_A_COST = 6_400_000_000
FAR_COST = 100_000_000
EXTRA_COST = 800_000_000
ONE_A_COST = 400_000_000
TAIL_COST = 200_000_000
AWAY_COST = 6_400_000_000
SPREAD_COST = 400_000_000
DIRECT_COST = 400_000_000
NEAR_COST = 400_000_000
VMEM = pl.BlockSpec(memory_space=pltpu.VMEM)
ROW_BY_ROW = (((1,), (1,)), ((), ()))


def route(block, target):
    pairs = []
    for q in range(N_SECTION):
        for d in range(N_DP):
            goal = target(q, d)
            if goal is not None:
                pairs.append((q * N_DP + d, goal[0] * N_DP + goal[1] % N_DP))
    return lax.ppermute(block, ("section", "dp"), pairs)


def to_core(q, d):
    return q ^ 1, d


def to_y(q, d):
    return q ^ 2, d


def along(q, d):
    return q, d + 1 - 2 * (q % 2)


def along_inside(q, d):
    last = RUN - 1 if q % 2 == 0 else 0
    return None if d % RUN == last else along(q, d)


def across(q, d):
    if q % 2 == 0:
        return (q, d + 2) if d % RUN == RUN - 2 else None
    return (q, d - 2) if d % RUN == 1 else None


def aside(q, d):
    step = 24 if q < 2 else 7
    if q % 2 == 1:
        steps = {RUN - 1: -step, RUN - 2: -24}
        return (q, d + steps[d % RUN]) if d % RUN in steps else None
    steps = {0: step, 1: 24}
    return (q ^ 1, d + steps[d % RUN]) if d % RUN in steps else None


def from_aside(q, d):
    if q % 2 == 0:
        return None
    step = 24 if q < 2 else 7
    goals = {
        RUN - 1 - step: (q ^ 1, d + step + 1),
        step: (q, d - step - 1),
        6: (q, d + 26),
        25: (q ^ 1, d - 26),
    }
    return goals.get(d % RUN)


def call(kernel, out_shape, flops, *operands):
    size = sum(x.size * x.dtype.itemsize for x in operands)
    return pl.pallas_call(
        kernel,
        out_shape=out_shape,
        in_specs=[pl.BlockSpec(memory_space=pltpu.SMEM) if x.ndim == 1 else VMEM for x in operands],
        out_specs=jax.tree.map(lambda _: VMEM, out_shape),
        cost_estimate=pl.CostEstimate(flops=flops, bytes_accessed=size, transcendentals=0),
        compiler_params=pltpu.CompilerParams(vmem_limit_bytes=16 * 2**20),
    )(*operands)


def normalise(rows):
    values = rows.astype(F32)
    inverse = lax.rsqrt(jnp.sum(values * values, axis=1, keepdims=True) + 1e-06)
    return (values * inverse).astype(BF16), inverse


def student_kernel(s_ref, unit_ref, inv_ref):
    unit_ref[...], inv_ref[...] = normalise(s_ref[...])


def both_kernel(unit_s, t_ref, unit_ref):
    unit_ref[:ROWS, :] = unit_s[...]
    unit_ref[ROWS:, :] = normalise(t_ref[...])[0]


def unit_rows(student, teacher):
    shape = jax.ShapeDtypeStruct
    outs = (shape((ROWS, D), BF16), shape((ROWS, 1), F32))
    unit_s, inv = call(student_kernel, outs, START_COST, student)
    return call(both_kernel, shape((2 * ROWS, D), BF16), 5 * ROWS * D, unit_s, teacher), inv


def stack(blocks, part):
    return jnp.concatenate([x[part * ROWS : (part + 1) * ROWS, :] for x in blocks], axis=0)


def terms(parts, rows, own_first):
    s_rows, t_rows = stack(rows, 0), stack(rows, 1)
    diff = lax.dot_general(stack(parts, 0), s_rows, ROW_BY_ROW, preferred_element_type=F32)
    diff = diff - lax.dot_general(stack(parts, 1), t_rows, ROW_BY_ROW, preferred_element_type=F32)
    if own_first:
        diff = jnp.concatenate([2.0 * diff[:, :ROWS], diff[:, ROWS:]], axis=1)
    return jnp.dot(diff.astype(BF16), s_rows, preferred_element_type=F32)


def hold_kernel(block, out_ref):
    out_ref[...] = block[...]


def next_kernel(flag, one_b, near_b, rows_ref):
    rows_ref[...] = one_b[...] + jnp.where(flag[0] == 1, near_b[...], jnp.zeros_like(near_b))


def extra_kernel(flag, near_b, direct, rows_ref):
    rows_ref[...] = direct[...] + jnp.where(flag[0] == 1, jnp.zeros_like(near_b), near_b[...])


def first_kernel(one, other, own, one_a, one_b, two_a, sum_ref):
    sum_ref[...] = terms([one, other], [own, one_a, one_b, two_a], True)


def final_kernel(one, other, two, extra, old_ref, keep_ref, send_ref):
    total = old_ref[...] + terms([one, other], [two, extra], False)
    keep_ref[...] = total[:ROWS, :]
    send_ref[...] = total[ROWS:, :].astype(BF16)


def far_kernel(keep, got, send_ref):
    send_ref[...] = (keep[...] + got[...].astype(F32)).astype(BF16)


def last_kernel(unit, inv, keep, got, got_far, out_hbm, out_ref, sems):
    part = ROWS // PARTS
    copies = []
    for i in range(PARTS):
        here = pl.ds(i * part, part)
        total = keep[here, :] + got[here, :].astype(F32) + got_far[here, :].astype(F32)
        unit_f = unit[here, :].astype(F32)
        along_unit = jnp.sum(unit_f * total, axis=1, keepdims=True)
        out_ref[here, :] = (D / 2.0 * inv[here, :] * (total - unit_f * along_unit)).astype(BF16)
        copies.append(pltpu.make_async_copy(out_ref.at[here], out_hbm.at[here], sems.at[i]))
        copies[i].start()
    for copy in copies:
        copy.wait()


def last(*operands):
    return pl.pallas_call(
        last_kernel,
        out_shape=jax.ShapeDtypeStruct((ROWS, D), BF16),
        in_specs=[VMEM] * len(operands),
        out_specs=pl.BlockSpec(memory_space=pl.ANY),
        scratch_shapes=[pltpu.VMEM((ROWS, D), BF16), pltpu.SemaphoreType.DMA((PARTS,))],
        cost_estimate=pl.CostEstimate(flops=8 * ROWS * D, bytes_accessed=12 * ROWS * D, transcendentals=0),
        compiler_params=pltpu.CompilerParams(vmem_limit_bytes=16 * 2**20),
    )(*operands)


def after(block, *others):
    return lax.optimization_barrier((block, *others))[0]


def hold(block, cost):
    return call(hold_kernel, jax.ShapeDtypeStruct(block.shape, block.dtype), cost, block)


def on_device(student, teacher):
    shape = jax.ShapeDtypeStruct
    quarter_f, quarter_h = shape((ROWS, D), F32), shape((ROWS, D), BF16)
    half, both = shape((2 * ROWS, D), F32), shape((2 * ROWS, D), BF16)
    gram = 2 * 3 * 2 * ROWS * ROWS * D
    own, inv = unit_rows(student, teacher)
    one_a = hold(route(own, along), ONE_A_COST)
    spread = hold(route(own, aside), SPREAD_COST)
    direct = hold(route(own, across), DIRECT_COST)
    far = hold(route(after(own, spread), to_y), FAR_COST)
    sib = route(own, to_core)
    one_b = route(sib, along_inside)
    near_b = route(spread, from_aside)
    core = lax.axis_index("section") % 2
    place = lax.axis_index("dp") % RUN
    flag = (place == core * (RUN - 1)).astype(jnp.int32).reshape(1)
    one_b = call(next_kernel, both, NEXT_COST, flag, one_b, near_b)
    extra = call(extra_kernel, both, EXTRA_COST, flag, near_b, direct)
    two_a = hold(route(one_a, along_inside), TWO_A_COST)
    two_b = route(one_b, along_inside)
    near_sum = call(first_kernel, half, NEAR_COST, own, sib, own, one_a, after(one_b, far), two_a)
    cross = route(after(far, one_b, extra), to_core)
    away_sum = call(first_kernel, half, AWAY_COST, far, cross, own, one_a, one_b, two_a)
    keep_far, send_far = call(
        final_kernel, (quarter_f, quarter_h), FINAL_COST, far, cross, two_b, extra, away_sum
    )
    got_far = route(send_far, to_core)
    send_far = call(far_kernel, quarter_h, ROWS * D, keep_far, got_far)
    got_far = hold(route(send_far, to_y), TAIL_COST)
    keep, send = call(final_kernel, (quarter_f, quarter_h), gram, own, sib, two_b, extra, near_sum)
    got = route(after(send, send_far), to_core)
    return last(own, inv, keep, got, got_far)


def solution(mesh):
    placed = (P(("section", "dp"), None), P(("section", "dp"), None))
    return jax.shard_map(
        on_device, mesh=mesh, in_specs=placed, out_specs=P(("section", "dp"), None), check_vma=False
    )
```

```python
import jax
import jax.numpy as jnp
from jax import lax
from jax.experimental import pallas as pl
from jax.experimental.pallas import tpu as pltpu
from jax.sharding import PartitionSpec as P

D = 1024
ROWS = 128
N_SECTION = 4
N_DP = 128
RUN = 32
PARTS = 4
F32 = jnp.float32
BF16 = jnp.bfloat16
START_COST = 1
NEXT_COST = 400_000_000
FINAL_COST = 400_000_000
TWO_A_COST = 6_400_000_000
FAR_COST = 100_000_000
EXTRA_COST = 800_000_000
ONE_A_COST = 400_000_000
TAIL_COST = 200_000_000
AWAY_COST = 6_400_000_000
DIRECT_COST = 400_000_000
NEAR_COST = 400_000_000
VMEM = pl.BlockSpec(memory_space=pltpu.VMEM)
ROW_BY_ROW = (((1,), (1,)), ((), ()))


def route(block, target):
    pairs = []
    for q in range(N_SECTION):
        for d in range(N_DP):
            goal = target(q, d)
            if goal is not None:
                pairs.append((q * N_DP + d, goal[0] * N_DP + goal[1] % N_DP))
    return lax.ppermute(block, ("section", "dp"), pairs)


def to_core(q, d):
    return q ^ 1, d


def to_y(q, d):
    return q ^ 2, d


def along(q, d):
    return q, d + 1 - 2 * (q % 2)


def along_inside(q, d):
    last = RUN - 1 if q % 2 == 0 else 0
    return None if d % RUN == last else along(q, d)


def across(q, d):
    if q % 2 == 0:
        return (q, d + 2) if d % RUN == RUN - 2 else None
    return (q, d - 2) if d % RUN == 1 else None


def aside(q, d):
    step = 24 if q < 2 else 7
    if q % 2 == 1:
        steps = {RUN - 1: -step, RUN - 2: -24}
        return (q, d + steps[d % RUN]) if d % RUN in steps else None
    steps = {0: step, 1: 24}
    return (q ^ 1, d + steps[d % RUN]) if d % RUN in steps else None


def from_aside(q, d):
    if q % 2 == 0:
        return None
    step = 24 if q < 2 else 7
    goals = {
        RUN - 1 - step: (q ^ 1, d + step + 1),
        step: (q, d - step - 1),
        6: (q, d + 26),
        25: (q ^ 1, d - 26),
    }
    return goals.get(d % RUN)


def call(kernel, out_shape, flops, *operands):
    size = sum(x.size * x.dtype.itemsize for x in operands)
    return pl.pallas_call(
        kernel,
        out_shape=out_shape,
        in_specs=[pl.BlockSpec(memory_space=pltpu.SMEM) if x.ndim == 1 else VMEM for x in operands],
        out_specs=jax.tree.map(lambda _: VMEM, out_shape),
        cost_estimate=pl.CostEstimate(flops=flops, bytes_accessed=size, transcendentals=0),
        compiler_params=pltpu.CompilerParams(vmem_limit_bytes=16 * 2**20),
    )(*operands)


def normalise(rows):
    values = rows.astype(F32)
    inverse = lax.rsqrt(jnp.sum(values * values, axis=1, keepdims=True) + 1e-06)
    return (values * inverse).astype(BF16), inverse


def student_kernel(s_ref, unit_ref, inv_ref):
    unit_ref[...], inv_ref[...] = normalise(s_ref[...])


def both_kernel(unit_s, t_ref, unit_ref):
    unit_ref[:ROWS, :] = unit_s[...]
    unit_ref[ROWS:, :] = normalise(t_ref[...])[0]


def unit_rows(student, teacher):
    shape = jax.ShapeDtypeStruct
    outs = (shape((ROWS, D), BF16), shape((ROWS, 1), F32))
    unit_s, inv = call(student_kernel, outs, START_COST, student)
    return call(both_kernel, shape((2 * ROWS, D), BF16), 5 * ROWS * D, unit_s, teacher), inv


def stack(blocks, part):
    return jnp.concatenate([x[part * ROWS : (part + 1) * ROWS, :] for x in blocks], axis=0)


def terms(parts, rows, own_first):
    s_rows, t_rows = stack(rows, 0), stack(rows, 1)
    diff = lax.dot_general(stack(parts, 0), s_rows, ROW_BY_ROW, preferred_element_type=F32)
    diff = diff - lax.dot_general(stack(parts, 1), t_rows, ROW_BY_ROW, preferred_element_type=F32)
    if own_first:
        diff = jnp.concatenate([2.0 * diff[:, :ROWS], diff[:, ROWS:]], axis=1)
    return jnp.dot(diff.astype(BF16), s_rows, preferred_element_type=F32)


def hold_kernel(block, out_ref):
    out_ref[...] = block[...]


def next_kernel(flag, one_b, near_b, rows_ref):
    rows_ref[...] = one_b[...] + jnp.where(flag[0] == 1, near_b[...], jnp.zeros_like(near_b))


def extra_kernel(flag, near_b, direct, rows_ref):
    rows_ref[...] = direct[...] + jnp.where(flag[0] == 1, jnp.zeros_like(near_b), near_b[...])


def first_kernel(one, other, own, one_a, one_b, two_a, sum_ref):
    sum_ref[...] = terms([one, other], [own, one_a, one_b, two_a], True)


def final_kernel(one, other, two, extra, old_ref, keep_ref, send_ref):
    total = old_ref[...] + terms([one, other], [two, extra], False)
    keep_ref[...] = total[:ROWS, :]
    send_ref[...] = total[ROWS:, :].astype(BF16)


def far_kernel(keep, got, send_ref):
    send_ref[...] = (keep[...] + got[...].astype(F32)).astype(BF16)


def last_kernel(unit, inv, keep, got, got_far, out_hbm, out_ref, sems):
    part = ROWS // PARTS
    copies = []
    for i in range(PARTS):
        here = pl.ds(i * part, part)
        total = keep[here, :] + got[here, :].astype(F32) + got_far[here, :].astype(F32)
        unit_f = unit[here, :].astype(F32)
        along_unit = jnp.sum(unit_f * total, axis=1, keepdims=True)
        out_ref[here, :] = (D / 2.0 * inv[here, :] * (total - unit_f * along_unit)).astype(BF16)
        copies.append(pltpu.make_async_copy(out_ref.at[here], out_hbm.at[here], sems.at[i]))
        copies[i].start()
    for copy in copies:
        copy.wait()


def last(*operands):
    return pl.pallas_call(
        last_kernel,
        out_shape=jax.ShapeDtypeStruct((ROWS, D), BF16),
        in_specs=[VMEM] * len(operands),
        out_specs=pl.BlockSpec(memory_space=pl.ANY),
        scratch_shapes=[pltpu.VMEM((ROWS, D), BF16), pltpu.SemaphoreType.DMA((PARTS,))],
        cost_estimate=pl.CostEstimate(flops=8 * ROWS * D, bytes_accessed=12 * ROWS * D, transcendentals=0),
        compiler_params=pltpu.CompilerParams(vmem_limit_bytes=16 * 2**20),
    )(*operands)


def after(block, *others):
    return lax.optimization_barrier((block, *others))[0]


def hold(block, cost):
    return call(hold_kernel, jax.ShapeDtypeStruct(block.shape, block.dtype), cost, block)


def on_device(student, teacher):
    shape = jax.ShapeDtypeStruct
    quarter_f, quarter_h = shape((ROWS, D), F32), shape((ROWS, D), BF16)
    half, both = shape((2 * ROWS, D), F32), shape((2 * ROWS, D), BF16)
    gram = 2 * 3 * 2 * ROWS * ROWS * D
    own, inv = unit_rows(student, teacher)
    one_a = hold(route(own, along), ONE_A_COST)
    spread = route(own, aside)
    direct = hold(route(own, across), DIRECT_COST)
    far = hold(route(after(own, spread), to_y), FAR_COST)
    sib = route(own, to_core)
    one_b = route(sib, along_inside)
    near_b = route(spread, from_aside)
    core = lax.axis_index("section") % 2
    place = lax.axis_index("dp") % RUN
    flag = (place == core * (RUN - 1)).astype(jnp.int32).reshape(1)
    one_b = call(next_kernel, both, NEXT_COST, flag, one_b, near_b)
    extra = call(extra_kernel, both, EXTRA_COST, flag, near_b, direct)
    two_a = hold(route(one_a, along_inside), TWO_A_COST)
    two_b = route(one_b, along_inside)
    near_sum = call(first_kernel, half, NEAR_COST, own, sib, own, one_a, after(one_b, far), two_a)
    cross = route(after(far, one_b, extra), to_core)
    away_sum = call(first_kernel, half, AWAY_COST, far, cross, own, one_a, one_b, two_a)
    keep_far, send_far = call(
        final_kernel, (quarter_f, quarter_h), FINAL_COST, far, cross, two_b, extra, away_sum
    )
    got_far = route(send_far, to_core)
    send_far = call(far_kernel, quarter_h, ROWS * D, keep_far, got_far)
    got_far = hold(route(send_far, to_y), TAIL_COST)
    keep, send = call(final_kernel, (quarter_f, quarter_h), gram, own, sib, two_b, extra, near_sum)
    got = route(after(send, send_far), to_core)
    return last(own, inv, keep, got, got_far)


def solution(mesh):
    placed = (P(("section", "dp"), None), P(("section", "dp"), None))
    return jax.shard_map(
        on_device, mesh=mesh, in_specs=placed, out_specs=P(("section", "dp"), None), check_vma=False
    )
```
